32 devices in a mesh: groups: 2 (over y), col: 8 (over z, x), row: 2 (over core).
Axes of the slice: x: 2, y: 2, z: 4, core: 2. Of those that a mesh axis runs over, the one named last changes fastest.
Arguments:
- tokens: bfloat16 [640, 8192], P(('groups', 'row'), 'col'), parts along dimension 0, may hold values from -6 to 6
- gate_weight: bfloat16 [8192, 2, 13312], P('row', None, 'col'), may hold values from -0.0625 to 0.0625
- up_weight: bfloat16 [8192, 2, 13312], P('row', None, 'col'), may hold values from -0.0625 to 0.0625
- down_weight: bfloat16 [2, 13312, 8192], P('row', None, 'col'), may hold values from -0.0390625 to 0.0390625
Outputs:
- output_rows: bfloat16 [640, 8192], P(('groups', 'row'), 'col'), parts along dimension 0
The draws below stay inside these ranges and needn't reach their ends.
There are 2 independent parts, one for each index of `groups`. The reference program is written for one: setup_inputs(seed, part) draws one part's arguments, and reference() takes and returns one part's arrays. A program takes and returns all parts, laid end to end along the dimension named above; an argument that names none is the same for every part. Nothing has to cross between parts.
All inputs are finite; a program needn't handle non-finite values.
Results may differ from the reference program's by a relative error of at most 0.006.
Values may be sent and summed in bfloat16 or wider, within the bound.
A program may use at most 576 MiB of HBM per device.

```python
import jax
import jax.numpy as jnp

D = 8192
FF = 26624
TOKENS = 320
N_ROW = 2


def levels(rng, shape, pieces, least, top_value):
    level, own = 1.0, jax.random.fold_in(rng, 6)
    for axis_at, parts in pieces:
        draws = jnp.exp(jax.random.uniform(jax.random.fold_in(own, axis_at), (parts,), jnp.float32, least / len(pieces), top_value / len(pieces)))
        level = level * jnp.repeat(draws, shape[axis_at] // parts).reshape([-1 if axis == axis_at else 1 for axis in range(len(shape))])
    return level


def centred(rng, dims, scale, most, cuts=(), dtype=jnp.bfloat16):
    drawn = jax.random.normal(rng, dims, jnp.float32) * scale
    if len(cuts) > 0:
        drawn = levels(rng, dims, cuts, -0.22, 0.18) * drawn
    return jnp.clip(drawn, min=-most, max=most).astype(dtype)


def setup_inputs(seed: int = 0, part: int = 0) -> dict:
    key_list = jax.random.split(jax.random.key(seed), 5)
    part_splits = jax.random.split(jax.random.fold_in(key_list[4], part), 5)
    tokens = centred(part_splits[0], (TOKENS, D), 1.0, 6.0, ((0, 2), (1, 8)))
    gate_weight = centred(key_list[1], (D, N_ROW, FF // N_ROW), D ** -0.5, 0.0625, ((0, 2), (2, 8)))
    up_weight = centred(key_list[2], (D, N_ROW, FF // N_ROW), D ** -0.5, 0.0625, ((0, 2), (2, 8)))
    down_weight = centred(key_list[3], (N_ROW, FF // N_ROW, D), FF ** -0.5, 0.0390625, ((0, 2), (2, 8)))
    return {"tokens": tokens, "gate_weight": gate_weight, "up_weight": up_weight, "down_weight": down_weight}


def reference(tokens, gate_weight, up_weight, down_weight):
    gate_flat = gate_weight.reshape(gate_weight.shape[0], -1)
    up_flat = up_weight.reshape(up_weight.shape[0], -1)
    down_flat = down_weight.reshape(-1, down_weight.shape[2])
    gate_proj = jnp.dot(tokens, gate_flat, preferred_element_type=jnp.float32)
    up_proj = jnp.dot(tokens, up_flat, preferred_element_type=jnp.float32)
    hidden = (jax.nn.silu(gate_proj) * up_proj).astype(jnp.bfloat16)
    output_rows = jnp.dot(hidden, down_flat, preferred_element_type=jnp.float32)
    return output_rows.astype(jnp.bfloat16)
```

```python
import functools

import jax
import jax.numpy as jnp
from jax import lax
from jax.experimental import pallas as pl
from jax.experimental.pallas import tpu as pltpu
from jax.sharding import PartitionSpec as P

BF16, F32 = jnp.bfloat16, jnp.float32
LANES = 128
TOK_PARTS = 2
W_SLOTS = 3
D_SLOTS = 4
STEP = 512


def plain(tokens, gate_weight, up_weight, down_weight):
    row = lax.axis_index("row")
    features = lax.all_gather(tokens, "col", axis=1, tiled=True)
    features = lax.all_gather(features, "row", axis=0, tiled=True)
    depth = gate_weight.shape[0]
    features = lax.dynamic_slice_in_dim(features, row * depth, depth, 1)

    def project(weight):
        part = jnp.einsum("td,dbu->btu", features, weight, preferred_element_type=F32)
        return lax.psum_scatter(part, "row", scatter_dimension=0, tiled=True)[0]

    hidden = (jax.nn.silu(project(gate_weight)) * project(up_weight)).astype(BF16)
    hidden = lax.all_gather(hidden, "col", axis=1, tiled=True)
    part = jnp.dot(hidden, down_weight[0], preferred_element_type=F32)
    return lax.psum_scatter(part, "row", scatter_dimension=0, tiled=True).astype(BF16)


def kernel(n_z, chunks, tok_ref, gate_ref, up_ref, down_ref, out_ref,
           tokr, tokp, spread, wg, wu, pacc, own, psend, precv, hid, acc, wd, osend, orecv,
           w_sem, tp_send, tp_recv, tr_send, tr_recv, p_send, p_recv, h_send, h_recv, d_sem, o_send, o_recv, own_sem):
    col, r = lax.axis_index("col"), lax.axis_index("row")
    z, x = col // 2, col % 2
    peer = 1 - r
    above, below, across = col + 2, col - 2, z * 2 + 1 - x
    has_up, has_down = z < n_z - 1, z > 0
    rows = tok_ref.shape[0]
    both = 2 * rows
    wide = tok_ref.shape[1]
    piece = wide // TOK_PARTS
    half = n_z
    depth = gate_ref.shape[0]
    mesh_id = pl.DeviceIdType.MESH

    def weight_copies(k):
        slot = lax.rem(k, W_SLOTS)
        cols = pl.ds(pl.multiple_of(k * LANES, LANES), LANES)
        return (pltpu.make_async_copy(gate_ref.at[:, :, cols], wg.at[slot], w_sem.at[slot, 0]),
                pltpu.make_async_copy(up_ref.at[:, :, cols], wu.at[slot], w_sem.at[slot, 1]))

    for k in range(W_SLOTS - 1):
        for copy in weight_copies(jnp.int32(k)):
            copy.start()

    barrier = pltpu.get_barrier_semaphore()
    pl.semaphore_signal(barrier, inc=1, device_id={"row": peer}, device_id_type=mesh_id)
    pl.semaphore_signal(barrier, inc=1, device_id={"col": across}, device_id_type=mesh_id)

    @pl.when(has_up)
    def _():
        pl.semaphore_signal(barrier, inc=1, device_id={"col": above}, device_id_type=mesh_id)

    @pl.when(has_down)
    def _():
        pl.semaphore_signal(barrier, inc=1, device_id={"col": below}, device_id_type=mesh_id)

    pl.semaphore_wait(barrier, 2 + has_up.astype(jnp.int32) + has_down.astype(jnp.int32))

    def block(buf, send, recv, unit, k, way, to):
        return pltpu.make_async_remote_copy(
            src_ref=buf.at[unit, k], dst_ref=buf.at[unit, k], send_sem=send.at[way, k],
            recv_sem=recv.at[unit, k], device_id={"col": to}, device_id_type=mesh_id)

    UP, DOWN, XL, XU = 0, 1, 2, 3

    def send_own(buf, send, recv, k):
        @pl.when(has_up)
        def _():
            block(buf, send, recv, col, k, UP, above).start()

        @pl.when(has_down)
        def _():
            block(buf, send, recv, col, k, DOWN, below).start()

        block(buf, send, recv, col, k, XL, across).start()

    def relay(buf, send, recv, s, k, arrived):
        lower, upper = col - 2 * s, col + 2 * s

        @pl.when(z - s >= 0)
        def _():
            block(buf, send, recv, lower, k, XL, across).wait_recv()

            @pl.when(has_up)
            def _():
                copy = block(buf, send, recv, lower, k, UP, above)
                copy.wait_send()
                copy.start()

            copy = block(buf, send, recv, lower, k, XL, across)
            copy.wait_send()
            copy.start()
            arrived(lower, k, 0)

        @pl.when(z + s < n_z)
        def _():
            block(buf, send, recv, upper, k, XU, across).wait_recv()

            @pl.when(has_down)
            def _():
                copy = block(buf, send, recv, upper, k, DOWN, below)
                copy.wait_send()
                copy.start()

            copy = block(buf, send, recv, upper, k, XU, across)

            @pl.when(s > 1)
            def _():
                copy.wait_send()

            copy.start()
            arrived(upper, k, 1)

        t = s - 1
        xl, xu = across - 2 * t, across + 2 * t

        @pl.when(z - t >= 0)
        def _():
            block(buf, send, recv, xl, k, XL, across).wait_recv()
            arrived(xl, k, 2)

        @pl.when((t > 0) & (z + t < n_z))
        def _():
            block(buf, send, recv, xu, k, XL, across).wait_recv()
            arrived(xu, k, 3)

    def drain(buf, send, recv, k):
        @pl.when(has_up)
        def _():
            block(buf, send, recv, col, k, UP, above).wait_send()
            block(buf, send, recv, col, k, XU, across).wait_send()

        @pl.when(has_down)
        def _():
            block(buf, send, recv, col, k, DOWN, below).wait_send()

        block(buf, send, recv, col, k, XL, across).wait_send()

    def to_peer(unit, k):
        at = lax.rem(unit, half)
        return pltpu.make_async_remote_copy(
            src_ref=tokr.at[unit, k], dst_ref=tokp.at[at, k], send_sem=tp_send.at[at, k],
            recv_sem=tp_recv.at[at, k], device_id={"row": peer}, device_id_type=mesh_id)

    def token_arrived(unit, k, j):
        @pl.when(unit // half != r)
        def _():
            to_peer(unit, k).start()

    for k in range(TOK_PARTS):
        copy = pltpu.make_async_copy(tok_ref.at[:, pl.ds(k * piece, piece)], tokr.at[col, k], own_sem.at[k])
        copy.start()
    for k in range(TOK_PARTS):
        pltpu.make_async_copy(tok_ref.at[:, pl.ds(k * piece, piece)], tokr.at[col, k], own_sem.at[k]).wait()
        send_own(tokr, tr_send, tr_recv, k)
        token_arrived(col, k, 0)

    def token_step(i, carry):
        relay(tokr, tr_send, tr_recv, i // TOK_PARTS + 1, lax.rem(i, TOK_PARTS), token_arrived)
        return carry

    lax.fori_loop(0, n_z * TOK_PARTS, token_step, 0)

    source = lax.broadcasted_iota(jnp.int32, (LANES, 2 * LANES), 0)
    place = lax.broadcasted_iota(jnp.int32, (LANES, 2 * LANES), 1)
    picks = [jnp.where(place == 2 * source + b, 1.0, 0.0).astype(BF16) for b in range(2)]

    def spread_rows(src, at, k, first):
        for j in range(piece // LANES):
            value = src[:, j * LANES:(j + 1) * LANES]
            dst = pl.multiple_of(((at * TOK_PARTS + k) * (piece // LANES) + j) * 2 * LANES, 2 * LANES)
            for b in range(2):
                spread[pl.ds(pl.multiple_of(b * both + first, 16), rows), pl.ds(dst, 2 * LANES)] = jnp.dot(
                    value, picks[b], preferred_element_type=F32).astype(BF16)

    def spread_step(i, carry):
        at, k = i // TOK_PARTS, lax.rem(i, TOK_PARTS)
        unit = r * half + at
        spread_rows(tokr.at[unit, k], at, k, r * rows)
        to_peer(unit, k).wait_recv()
        spread_rows(tokp.at[at, k], at, k, peer * rows)
        to_peer(unit, k).wait_send()
        return carry

    lax.fori_loop(0, half * TOK_PARTS, spread_step, 0)
    for k in range(TOK_PARTS):
        drain(tokr, tr_send, tr_recv, k)

    def partial(k):
        return pltpu.make_async_remote_copy(
            src_ref=psend.at[k], dst_ref=precv.at[k], send_sem=p_send.at[k], recv_sem=p_recv.at[k],
            device_id={"row": peer}, device_id_type=mesh_id)

    def make_step(k, carry):
        @pl.when(k < chunks)
        def _():
            slot = lax.rem(k, W_SLOTS)

            @pl.when(k + W_SLOTS - 1 < chunks)
            def _():
                for copy in weight_copies(k + W_SLOTS - 1):
                    copy.start()

            for copy in weight_copies(k):
                copy.wait()
            pacc[...] = jnp.zeros_like(pacc)

            def contract(i, c):
                at = pl.ds(pl.multiple_of(i * STEP, STEP), STEP)
                gate = wg[slot, at].reshape(2 * STEP, LANES)
                up = wu[slot, at].reshape(2 * STEP, LANES)
                pacc[...] += jnp.dot(
                    spread[:, pl.ds(pl.multiple_of(i * 2 * STEP, 2 * STEP), 2 * STEP)],
                    jnp.concatenate([gate, up], axis=1), preferred_element_type=F32)
                return c

            lax.fori_loop(0, depth // STEP, contract, 0)
            psend[k] = pacc[pl.ds(pl.multiple_of(peer * both, 16), both), :].astype(BF16)
            partial(k).start()

        @pl.when(k > 0)
        def _():
            last = k - 1
            partial(last).wait_recv()
            total = own[...] + precv[last].astype(F32)
            gate, up = total[:, :LANES], total[:, LANES:]
            hid[col, last] = (gate / (1.0 + jnp.exp(-gate)) * up).astype(BF16)
            send_own(hid, h_send, h_recv, last)

        @pl.when(k < chunks)
        def _():
            own[...] = pacc[pl.ds(pl.multiple_of(r * both, 16), both), :]

        return carry

    lax.fori_loop(0, chunks + 1, make_step, 0)

    steps = n_z * chunks

    def unit_of(s, j):
        t = s - 1
        if j == 0:
            return z - s >= 0, col - 2 * s
        if j == 1:
            return z + s < n_z, col + 2 * s
        if j == 2:
            return z - t >= 0, across - 2 * t
        first = t == 0
        return first | (z + t < n_z), jnp.where(first, col, across + 2 * t)

    def down_copy(unit, k, slot, j):
        at = pl.multiple_of((unit * chunks + k) * LANES, LANES)
        return pltpu.make_async_copy(down_ref.at[0, pl.ds(at, LANES), :], wd.at[slot, j], d_sem.at[slot, j])

    def fetch(i):
        s, k = i // chunks + 1, lax.rem(i, chunks)
        for j in range(4):
            valid, unit = unit_of(s, j)

            @pl.when(valid)
            def _(unit=unit, j=j):
                down_copy(unit, k, lax.rem(i, D_SLOTS), j).start()

    for i in range(D_SLOTS - 1):
        fetch(jnp.int32(i))
    acc[...] = jnp.zeros_like(acc)

    def down_step(i, carry):
        s, k = i // chunks + 1, lax.rem(i, chunks)
        slot = lax.rem(i, D_SLOTS)

        @pl.when(i + D_SLOTS - 1 < steps)
        def _():
            fetch(i + D_SLOTS - 1)

        def arrived(unit, k, j):
            down_copy(unit, k, slot, j).wait()
            acc[...] += jnp.dot(hid[unit, k], wd[slot, j], preferred_element_type=F32)

        relay(hid, h_send, h_recv, s, k, arrived)

        @pl.when(s == 1)
        def _():
            arrived(col, k, 3)

        return carry

    lax.fori_loop(0, steps, down_step, 0)

    osend[...] = acc[pl.ds(pl.multiple_of(peer * rows, 16), rows), :].astype(BF16)
    copy = pltpu.make_async_remote_copy(
        src_ref=osend, dst_ref=orecv, send_sem=o_send, recv_sem=o_recv,
        device_id={"row": peer}, device_id_type=mesh_id)
    copy.start()

    def finish(k, carry):
        drain(hid, h_send, h_recv, k)
        partial(k).wait_send()
        return carry

    lax.fori_loop(0, chunks, finish, 0)
    copy.wait()
    out_ref[...] = (acc[pl.ds(pl.multiple_of(r * rows, 16), rows), :] + orecv[...].astype(F32)).astype(BF16)


def fused(n_col, tokens, gate_weight, up_weight, down_weight):
    rows, wide = tokens.shape
    depth, _, units = gate_weight.shape
    chunks = units // LANES
    n_z = n_col // 2
    both = 2 * rows
    any_space = pl.BlockSpec(memory_space=pl.ANY)
    vmem = pl.BlockSpec(memory_space=pltpu.VMEM)
    dma = pltpu.SemaphoreType.DMA
    return pl.pallas_call(
        functools.partial(kernel, n_z, chunks),
        out_shape=jax.ShapeDtypeStruct((rows, down_weight.shape[2]), BF16),
        in_specs=[any_space] * 4,
        out_specs=vmem,
        scratch_shapes=[
            pltpu.VMEM((n_col, TOK_PARTS, rows, wide // TOK_PARTS), BF16),
            pltpu.VMEM((n_z, TOK_PARTS, rows, wide // TOK_PARTS), BF16),
            pltpu.VMEM((2 * both, 2 * depth), BF16),
            pltpu.VMEM((W_SLOTS, depth, 2, LANES), BF16),
            pltpu.VMEM((W_SLOTS, depth, 2, LANES), BF16),
            pltpu.VMEM((2 * both, 2 * LANES), F32),
            pltpu.VMEM((both, 2 * LANES), F32),
            pltpu.VMEM((chunks, both, 2 * LANES), BF16),
            pltpu.VMEM((chunks, both, 2 * LANES), BF16),
            pltpu.VMEM((n_col, chunks, both, LANES), BF16),
            pltpu.VMEM((both, down_weight.shape[2]), F32),
            pltpu.VMEM((D_SLOTS, 4, LANES, down_weight.shape[2]), BF16),
            pltpu.VMEM((rows, down_weight.shape[2]), BF16),
            pltpu.VMEM((rows, down_weight.shape[2]), BF16),
            dma((W_SLOTS, 2)),
            dma((n_z, TOK_PARTS)), dma((n_z, TOK_PARTS)),
            dma((4, TOK_PARTS)), dma((n_col, TOK_PARTS)),
            dma((chunks,)), dma((chunks,)),
            dma((4, chunks)), dma((n_col, chunks)),
            dma((D_SLOTS, 4)),
            dma, dma,
            dma((TOK_PARTS,)),
        ],
        compiler_params=pltpu.CompilerParams(
            collective_id=0, has_side_effects=True, vmem_limit_bytes=58 * 2**20),
    )(tokens, gate_weight, up_weight, down_weight)


def solution(mesh):
    n_col = mesh.shape["col"]

    def local(tokens, gate_weight, up_weight, down_weight):
        rows, wide = tokens.shape
        depth, blocks, units = gate_weight.shape
        fits = (n_col == 8 and mesh.shape["row"] == 2 and blocks == 2 and units % LANES == 0
                and rows % 16 == 0 and wide % (TOK_PARTS * LANES) == 0 and depth % STEP == 0
                and 2 * depth == n_col * wide)
        if fits:
            return fused(n_col, tokens, gate_weight, up_weight, down_weight)
        return plain(tokens, gate_weight, up_weight, down_weight)

    in_specs = (
        P(("groups", "row"), "col"),
        P("row", None, "col"),
        P("row", None, "col"),
        P("row", None, "col"),
    )
    out_specs = P(("groups", "row"), "col")
    return jax.shard_map(local, mesh=mesh, in_specs=in_specs, out_specs=out_specs, check_vma=False)
```

```python
import functools

import jax
import jax.numpy as jnp
from jax import lax
from jax.experimental import pallas as pl
from jax.experimental.pallas import tpu as pltpu
from jax.sharding import PartitionSpec as P

BF16, F32 = jnp.bfloat16, jnp.float32
LANES = 128
TOK_PARTS = 2
W_SLOTS = 3
D_SLOTS = 4
ACROSS = 2
LAG = 2
STEP = 4096


def plain(tokens, gate_weight, up_weight, down_weight):
    row = lax.axis_index("row")
    features = lax.all_gather(tokens, "col", axis=1, tiled=True)
    features = lax.all_gather(features, "row", axis=0, tiled=True)
    depth = gate_weight.shape[0]
    features = lax.dynamic_slice_in_dim(features, row * depth, depth, 1)

    def project(weight):
        part = jnp.einsum("td,dbu->btu", features, weight, preferred_element_type=F32)
        return lax.psum_scatter(part, "row", scatter_dimension=0, tiled=True)[0]

    hidden = (jax.nn.silu(project(gate_weight)) * project(up_weight)).astype(BF16)
    hidden = lax.all_gather(hidden, "col", axis=1, tiled=True)
    part = jnp.dot(hidden, down_weight[0], preferred_element_type=F32)
    return lax.psum_scatter(part, "row", scatter_dimension=0, tiled=True).astype(BF16)


def kernel(n_z, chunks, tok_ref, gate_ref, up_ref, down_ref, out_ref,
           tokr, tokp, spread, wg, wu, pacc, own, psend, precv, hid, acc, wd, osend, orecv,
           w_sem, tp_send, tp_recv, tr_send, tr_recv, p_send, p_recv, h_send, h_recv, d_sem, o_send, o_recv, own_sem):
    col, r = lax.axis_index("col"), lax.axis_index("row")
    z, x = col // 2, col % 2
    peer = 1 - r
    above, below, across = col + 2, col - 2, z * 2 + 1 - x
    has_up, has_down = z < n_z - 1, z > 0
    rows = tok_ref.shape[0]
    both = 2 * rows
    wide = tok_ref.shape[1]
    piece = wide // TOK_PARTS
    half = n_z
    depth = gate_ref.shape[0]
    mesh_id = pl.DeviceIdType.MESH

    def weight_copies(k):
        slot = lax.rem(k, W_SLOTS)
        cols = pl.ds(pl.multiple_of(k * LANES, LANES), LANES)
        return (pltpu.make_async_copy(gate_ref.at[:, :, cols], wg.at[slot], w_sem.at[slot, 0]),
                pltpu.make_async_copy(up_ref.at[:, :, cols], wu.at[slot], w_sem.at[slot, 1]))

    for k in range(W_SLOTS - 1):
        for copy in weight_copies(jnp.int32(k)):
            copy.start()

    barrier = pltpu.get_barrier_semaphore()
    pl.semaphore_signal(barrier, inc=1, device_id={"row": peer}, device_id_type=mesh_id)
    pl.semaphore_signal(barrier, inc=1, device_id={"col": across}, device_id_type=mesh_id)

    @pl.when(has_up)
    def _():
        pl.semaphore_signal(barrier, inc=1, device_id={"col": above}, device_id_type=mesh_id)

    @pl.when(has_down)
    def _():
        pl.semaphore_signal(barrier, inc=1, device_id={"col": below}, device_id_type=mesh_id)

    pl.semaphore_wait(barrier, 2 + has_up.astype(jnp.int32) + has_down.astype(jnp.int32))

    def block(buf, send, recv, unit, k, way, to):
        return pltpu.make_async_remote_copy(
            src_ref=buf.at[unit, k], dst_ref=buf.at[unit, k], send_sem=send.at[way, k],
            recv_sem=recv.at[unit, k], device_id={"col": to}, device_id_type=mesh_id)

    UP, DOWN, XL, XU, UP2, DOWN2 = 0, 1, 2, 3, 4, 5

    def send_own(buf, send, recv, k):
        @pl.when(has_up)
        def _():
            block(buf, send, recv, col, k, UP, above).start()

        @pl.when(has_down)
        def _():
            block(buf, send, recv, col, k, DOWN, below).start()

        block(buf, send, recv, col, k, XL, across).start()

    def relay(buf, send, recv, s, k, arrived, turned):
        lower, upper = col - 2 * s, col + 2 * s

        @pl.when(z - s >= 0)
        def _():
            block(buf, send, recv, lower, k, XL, across).wait_recv()

            @pl.when(has_up)
            def _():
                copy = block(buf, send, recv, lower, k, UP, above)
                copy.wait_send()
                copy.start()

            @pl.when(k >= turned)
            def _():
                copy = block(buf, send, recv, lower, k, XL, across)
                copy.wait_send()
                copy.start()

            arrived(lower, k, 0)

        @pl.when(z + s < n_z)
        def _():
            block(buf, send, recv, upper, k, XU, across).wait_recv()

            @pl.when(has_down)
            def _():
                copy = block(buf, send, recv, upper, k, DOWN, below)
                copy.wait_send()
                copy.start()

            @pl.when(k >= turned)
            def _():
                copy = block(buf, send, recv, upper, k, XU, across)

                @pl.when(s > 1)
                def _():
                    copy.wait_send()

                copy.start()

            arrived(upper, k, 1)

        t = s - 1
        xl, xu = across - 2 * t, across + 2 * t

        @pl.when(z - t >= 0)
        def _():
            block(buf, send, recv, xl, k, XL, across).wait_recv()

            @pl.when((k < turned) & has_up)
            def _():
                copy = block(buf, send, recv, xl, k, UP2, above)

                @pl.when(t > 0)
                def _():
                    copy.wait_send()

                copy.start()

            @pl.when((k < turned) & has_down & (t == 0))
            def _():
                block(buf, send, recv, xl, k, DOWN2, below).start()

            arrived(xl, k, 2)

        @pl.when((t > 0) & (z + t < n_z))
        def _():
            block(buf, send, recv, xu, k, XL, across).wait_recv()

            @pl.when((k < turned) & has_down)
            def _():
                copy = block(buf, send, recv, xu, k, DOWN2, below)
                copy.wait_send()
                copy.start()

            arrived(xu, k, 3)

    def drain(buf, send, recv, k, turned):
        @pl.when(has_up)
        def _():
            block(buf, send, recv, col, k, UP, above).wait_send()

        @pl.when(has_up & (k >= turned))
        def _():
            block(buf, send, recv, col, k, XU, across).wait_send()

        @pl.when(has_up & (k < turned))
        def _():
            block(buf, send, recv, col, k, UP2, above).wait_send()

        @pl.when(has_down)
        def _():
            block(buf, send, recv, col, k, DOWN, below).wait_send()

        @pl.when(has_down & (k < turned))
        def _():
            block(buf, send, recv, col, k, DOWN2, below).wait_send()

        block(buf, send, recv, col, k, XL, across).wait_send()

    def to_peer(unit, k):
        at = lax.rem(unit, half)
        return pltpu.make_async_remote_copy(
            src_ref=tokr.at[unit, k], dst_ref=tokp.at[at, k], send_sem=tp_send.at[at, k],
            recv_sem=tp_recv.at[at, k], device_id={"row": peer}, device_id_type=mesh_id)

    def token_arrived(unit, k, j):
        @pl.when(unit // half != r)
        def _():
            to_peer(unit, k).start()

    for k in range(TOK_PARTS):
        copy = pltpu.make_async_copy(tok_ref.at[:, pl.ds(k * piece, piece)], tokr.at[col, k], own_sem.at[k])
        copy.start()
    for k in range(TOK_PARTS):
        pltpu.make_async_copy(tok_ref.at[:, pl.ds(k * piece, piece)], tokr.at[col, k], own_sem.at[k]).wait()
        send_own(tokr, tr_send, tr_recv, k)
        token_arrived(col, k, 0)

    def token_step(i, carry):
        relay(tokr, tr_send, tr_recv, i // TOK_PARTS + 1, lax.rem(i, TOK_PARTS), token_arrived, 0)
        return carry

    lax.fori_loop(0, n_z * TOK_PARTS, token_step, 0)

    source = lax.broadcasted_iota(jnp.int32, (LANES, 2 * LANES), 0)
    place = lax.broadcasted_iota(jnp.int32, (LANES, 2 * LANES), 1)
    picks = [jnp.where(place == 2 * source + b, 1.0, 0.0).astype(BF16) for b in range(2)]

    def spread_rows(src, at, k, first):
        for j in range(piece // LANES):
            value = src[:, j * LANES:(j + 1) * LANES]
            dst = pl.multiple_of(((at * TOK_PARTS + k) * (piece // LANES) + j) * 2 * LANES, 2 * LANES)
            for b in range(2):
                spread[pl.ds(pl.multiple_of(b * both + first, 16), rows), pl.ds(dst, 2 * LANES)] = jnp.dot(
                    value, picks[b], preferred_element_type=F32).astype(BF16)

    def spread_step(i, carry):
        at, k = i // TOK_PARTS, lax.rem(i, TOK_PARTS)
        unit = r * half + at
        spread_rows(tokr.at[unit, k], at, k, r * rows)
        to_peer(unit, k).wait_recv()
        spread_rows(tokp.at[at, k], at, k, peer * rows)
        to_peer(unit, k).wait_send()
        return carry

    lax.fori_loop(0, half * TOK_PARTS, spread_step, 0)
    for k in range(TOK_PARTS):
        drain(tokr, tr_send, tr_recv, k, 0)

    steps = n_z * chunks

    def unit_of(s, j):
        t = s - 1
        if j == 0:
            return z - s >= 0, col - 2 * s
        if j == 1:
            return z + s < n_z, col + 2 * s
        if j == 2:
            return z - t >= 0, across - 2 * t
        first = t == 0
        return first | (z + t < n_z), jnp.where(first, col, across + 2 * t)

    def down_copy(unit, k, slot, j):
        at = pl.multiple_of((unit * chunks + k) * LANES, LANES)
        return pltpu.make_async_copy(down_ref.at[0, pl.ds(at, LANES), :], wd.at[slot, j], d_sem.at[slot, j])

    def fetch(i):
        s, k = i // chunks + 1, lax.rem(i, chunks)
        for j in range(4):
            valid, unit = unit_of(s, j)

            @pl.when(valid)
            def _(unit=unit, j=j):
                down_copy(unit, k, lax.rem(i, D_SLOTS), j).start()

    for i in range(D_SLOTS - 1):
        fetch(jnp.int32(i))
    acc[...] = jnp.zeros_like(acc)

    def down_step(i, carry):
        s, k = i // chunks + 1, lax.rem(i, chunks)
        slot = lax.rem(i, D_SLOTS)

        @pl.when(i + D_SLOTS - 1 < steps)
        def _():
            fetch(i + D_SLOTS - 1)

        def arrived(unit, k, j):
            down_copy(unit, k, slot, j).wait()
            acc[...] += jnp.dot(hid[unit, k], wd[slot, j], preferred_element_type=F32)

        relay(hid, h_send, h_recv, s, k, arrived, ACROSS)

        @pl.when(s == 1)
        def _():
            arrived(col, k, 3)

        return carry

    def partial(k):
        return pltpu.make_async_remote_copy(
            src_ref=psend.at[k], dst_ref=precv.at[k], send_sem=p_send.at[k], recv_sem=p_recv.at[k],
            device_id={"row": peer}, device_id_type=mesh_id)

    def make_step(k, carry):
        @pl.when(k < chunks)
        def _():
            slot = lax.rem(k, W_SLOTS)

            @pl.when(k + W_SLOTS - 1 < chunks)
            def _():
                for copy in weight_copies(k + W_SLOTS - 1):
                    copy.start()

            for copy in weight_copies(k):
                copy.wait()
            pacc[...] = jnp.zeros_like(pacc)

            def contract(i, c):
                at = pl.ds(pl.multiple_of(i * STEP, STEP), STEP)
                gate = wg[slot, at].reshape(2 * STEP, LANES)
                up = wu[slot, at].reshape(2 * STEP, LANES)
                pacc[...] += jnp.dot(
                    spread[:, pl.ds(pl.multiple_of(i * 2 * STEP, 2 * STEP), 2 * STEP)],
                    jnp.concatenate([gate, up], axis=1), preferred_element_type=F32)
                return c

            lax.fori_loop(0, depth // STEP, contract, 0)
            psend[k] = pacc[pl.ds(pl.multiple_of(peer * both, 16), both), :].astype(BF16)
            partial(k).start()

        @pl.when(k > 0)
        def _():
            last = k - 1
            partial(last).wait_recv()
            total = own[...] + precv[last].astype(F32)
            gate, up = total[:, :LANES], total[:, LANES:]
            hid[col, last] = (gate / (1.0 + jnp.exp(-gate)) * up).astype(BF16)
            send_own(hid, h_send, h_recv, last)

        @pl.when(k < chunks)
        def _():
            own[...] = pacc[pl.ds(pl.multiple_of(r * both, 16), both), :]

        @pl.when(k > LAG)
        def _():
            down_step(k - 1 - LAG, 0)

        return carry

    lax.fori_loop(0, chunks + 1, make_step, 0)
    lax.fori_loop(chunks - LAG, steps, down_step, 0)

    osend[...] = acc[pl.ds(pl.multiple_of(peer * rows, 16), rows), :].astype(BF16)
    copy = pltpu.make_async_remote_copy(
        src_ref=osend, dst_ref=orecv, send_sem=o_send, recv_sem=o_recv,
        device_id={"row": peer}, device_id_type=mesh_id)
    copy.start()

    def finish(k, carry):
        drain(hid, h_send, h_recv, k, ACROSS)
        partial(k).wait_send()
        return carry

    lax.fori_loop(0, chunks, finish, 0)
    copy.wait()
    out_ref[...] = (acc[pl.ds(pl.multiple_of(r * rows, 16), rows), :] + orecv[...].astype(F32)).astype(BF16)


def fused(n_col, tokens, gate_weight, up_weight, down_weight):
    rows, wide = tokens.shape
    depth, _, units = gate_weight.shape
    chunks = units // LANES
    n_z = n_col // 2
    both = 2 * rows
    any_space = pl.BlockSpec(memory_space=pl.ANY)
    vmem = pl.BlockSpec(memory_space=pltpu.VMEM)
    dma = pltpu.SemaphoreType.DMA
    return pl.pallas_call(
        functools.partial(kernel, n_z, chunks),
        out_shape=jax.ShapeDtypeStruct((rows, down_weight.shape[2]), BF16),
        in_specs=[any_space] * 4,
        out_specs=vmem,
        scratch_shapes=[
            pltpu.VMEM((n_col, TOK_PARTS, rows, wide // TOK_PARTS), BF16),
            pltpu.VMEM((n_z, TOK_PARTS, rows, wide // TOK_PARTS), BF16),
            pltpu.VMEM((2 * both, 2 * depth), BF16),
            pltpu.VMEM((W_SLOTS, depth, 2, LANES), BF16),
            pltpu.VMEM((W_SLOTS, depth, 2, LANES), BF16),
            pltpu.VMEM((2 * both, 2 * LANES), F32),
            pltpu.VMEM((both, 2 * LANES), F32),
            pltpu.VMEM((chunks, both, 2 * LANES), BF16),
            pltpu.VMEM((chunks, both, 2 * LANES), BF16),
            pltpu.VMEM((n_col, chunks, both, LANES), BF16),
            pltpu.VMEM((both, down_weight.shape[2]), F32),
            pltpu.VMEM((D_SLOTS, 4, LANES, down_weight.shape[2]), BF16),
            pltpu.VMEM((rows, down_weight.shape[2]), BF16),
            pltpu.VMEM((rows, down_weight.shape[2]), BF16),
            dma((W_SLOTS, 2)),
            dma((n_z, TOK_PARTS)), dma((n_z, TOK_PARTS)),
            dma((6, TOK_PARTS)), dma((n_col, TOK_PARTS)),
            dma((chunks,)), dma((chunks,)),
            dma((6, chunks)), dma((n_col, chunks)),
            dma((D_SLOTS, 4)),
            dma, dma,
            dma((TOK_PARTS,)),
        ],
        compiler_params=pltpu.CompilerParams(
            collective_id=0, has_side_effects=True, vmem_limit_bytes=58 * 2**20),
    )(tokens, gate_weight, up_weight, down_weight)


def solution(mesh):
    n_col = mesh.shape["col"]

    def local(tokens, gate_weight, up_weight, down_weight):
        rows, wide = tokens.shape
        depth, blocks, units = gate_weight.shape
        fits = (n_col == 8 and mesh.shape["row"] == 2 and blocks == 2 and units % LANES == 0
                and rows % 16 == 0 and wide % (TOK_PARTS * LANES) == 0 and depth % STEP == 0
                and 2 * depth == n_col * wide)
        if fits:
            return fused(n_col, tokens, gate_weight, up_weight, down_weight)
        return plain(tokens, gate_weight, up_weight, down_weight)

    in_specs = (
        P(("groups", "row"), "col"),
        P("row", None, "col"),
        P("row", None, "col"),
        P("row", None, "col"),
    )
    out_specs = P(("groups", "row"), "col")
    return jax.shard_map(local, mesh=mesh, in_specs=in_specs, out_specs=out_specs, check_vma=False)
```
